512 devices in a mesh: dp: 4 (over x), row: 8 (over y_lo, core), col: 16 (over z, y_hi).
Axes of the slice: x: 4, y: 8 (y_hi: 2, y_lo: 4; y = y_hi * 4 + y_lo), z: 8, core: 2. Of those that a mesh axis runs over, the one named last changes fastest.
Arguments:
- tokens_window: bfloat16 [16384, 2048], P(('dp', 'row'), 'col'), parts along dimension 0, may hold values from -6 to 6
- weight_window: bfloat16 [2048, 24576], P('row', 'col'), may hold values from -0.125 to 0.125
- accumulated: float32 [16384, 24576], P(('dp', 'row'), 'col'), parts along dimension 0, may hold values from -6 to 6
Outputs:
- activated: bfloat16 [16384, 24576], P(('dp', 'row'), 'col'), parts along dimension 0
The draws below stay inside these ranges and needn't reach their ends.
There are 4 independent parts, one for each index of `dp`. The reference program is written for one: setup_inputs(seed, part) draws one part's arguments, and reference() takes and returns one part's arrays. A program takes and returns all parts, laid end to end along the dimension named above; an argument that names none is the same for every part. Nothing has to cross between parts.
All inputs are finite; a program needn't handle non-finite values.
Results may differ from the reference program's by a relative error of at most 0.001.
Values may be sent and summed in bfloat16 or wider, within the bound.
No kernel may reach another device: no remote copies, remote signals or barrier semaphores. Data moves between devices by JAX's collectives and lax.ppermute only.
A program may use at most 64 MiB of HBM per device.

```python
import jax
import jax.numpy as jnp

TOKENS = 4096
FF = 24576
KWIN = 2048


def block_scale(stream_key, shape, shards, smallest, top_value):
    gain, own = 1.0, jax.random.fold_in(stream_key, 6)
    for position, blocks in shards:
        draws = jnp.exp(jax.random.uniform(jax.random.fold_in(own, position), (blocks,), jnp.float32, smallest / len(shards), top_value / len(shards)))
        gain = gain * jnp.repeat(draws, shape[position] // blocks).reshape([-1 if axis == position else 1 for axis in range(len(shape))])
    return gain


def normal_values(rng, extent, scale, most, split=(), held_as=jnp.bfloat16):
    array = scale * jax.random.normal(rng, extent, jnp.float32)
    if split:
        array = array * block_scale(rng, extent, split, -0.22, 0.18)
    return jnp.clip(array, -most, most).astype(held_as)


def setup_inputs(seed: int = 0, part: int = 0) -> dict:
    arg_keys = jax.random.split(jax.random.key(seed), 4)
    own_keys = jax.random.split(jax.random.fold_in(arg_keys[3], part), 4)
    return {
        "tokens_window": normal_values(own_keys[0], (TOKENS, KWIN), 1.0, 6.0, ((0, 8), (1, 16))),
        "weight_window": normal_values(arg_keys[1], (KWIN, FF), KWIN ** -0.5, 0.125, ((0, 8), (1, 16))),
        "accumulated": normal_values(own_keys[2], (TOKENS, FF), 1.0, 6.0, ((0, 8), (1, 16)), jnp.float32),
    }


def reference(tokens_window, weight_window, accumulated):
    total = accumulated + jnp.dot(tokens_window, weight_window, preferred_element_type=jnp.float32)
    return jax.nn.gelu(total, approximate=True).astype(jnp.bfloat16)
```

```python
import functools

import jax
import jax.numpy as jnp
from jax import lax
from jax.experimental import pallas as pl
from jax.experimental.pallas import tpu as pltpu
from jax.sharding import PartitionSpec as P

AXES = ("dp", "row", "col")
X, YL, CORES, Z, YH = 4, 4, 2, 8, 2
TOK, KB, FF = 512, 256, 1536
Q = FF // X
HALF = KB // YH


def send(array, to):
    pairs = []
    for x in range(X):
        for yl in range(YL):
            for c in range(CORES):
                for z in range(Z):
                    for yh in range(YH):
                        x2, yl2, c2, z2, yh2 = to(x, yl, c, z, yh)
                        source = (x * YL * CORES + yl * CORES + c) * Z * YH + z * YH + yh
                        target = ((x2 % X) * YL * CORES + yl2 * CORES + c2) * Z * YH + (z2 % Z) * YH + yh2
                        pairs.append((source, target))
    return lax.ppermute(array, AXES, pairs)


def swap(array):
    return send(array, lambda x, yl, c, z, yh: (x, yl, 1 - c, z, yh))


def gelu(v):
    return 0.5 * v * (1.0 + jnp.tanh(0.7978845608028654 * (v + 0.044715 * (v * v * v))))


def kernel(place, *refs):
    (t, t1, t2, t3, vp, vm, p2, m2, w, sw, g, sg, x1, x2, x3, s1, s2, s3, acc, out,
     tokens, weights, sums, result, t_sem, w_sem, a_sem, o_sem) = refs
    d, yl, c, z, yh = (place[i] for i in range(5))

    def start(source, target, sem):
        copy = pltpu.make_async_copy(source, target, sem)
        copy.start()
        return copy

    t_copies = []
    parts = [(t, 0, 0, 0), (t1, 0, 0, 1), (t2, 0, 4, 0), (t3, 0, 4, 1)]
    for v, dz in ((vp, 1), (vm, 7)):
        parts += [(v, 0, dz, 0), (v, 1, dz, 1), (v, 2, dz + 4, 0), (v, 3, dz + 4, 1)]
    for v, dz in ((p2, 2), (m2, 6)):
        parts += [(v, 0, dz, 0), (v, 1, dz, 1)]
    for i, (ref, column, dz, dyh) in enumerate(parts):
        at = pl.multiple_of((lax.rem(z + dz, Z) * YH + (yh + dyh - 2 * yh * dyh)) * HALF, HALF)
        t_copies.append(start(ref.at[:, pl.ds(column * HALF, HALF)], tokens.at[:, pl.ds(at, HALF)], t_sem.at[i]))

    w_copies, a_copies = [], []
    for j, (mine, other) in enumerate(((g, sg), (x1, s1), (x2, s2), (x3, s3))):
        column = pl.multiple_of(lax.bitwise_xor(d, j) * Q, 128)
        a_copies.append(start(acc.at[:, pl.ds(column, Q)], sums.at[j], a_sem.at[j]))
        copies = []
        for side, (own, rest) in enumerate(((w, mine), (sw, other))):
            core = c if side == 0 else 1 - c
            for k in range(YL):
                row = pl.multiple_of((lax.bitwise_xor(yl, k) * CORES + core) * KB, KB)
                source = own.at[:, pl.ds(column, Q)] if k == 0 else rest.at[pl.ds((k - 1) * KB, KB), :]
                copies.append(start(source, weights.at[j, pl.ds(row, KB), :], w_sem.at[j * 8 + side * 4 + k]))
        w_copies.append(copies)

    for copy in t_copies:
        copy.wait()
    o_copies = []
    for j in range(X):
        for copy in w_copies[j]:
            copy.wait()
        a_copies[j].wait()
        total = sums[j] + jnp.dot(tokens[...], weights[j], preferred_element_type=jnp.float32)
        result[j] = gelu(total).astype(jnp.bfloat16)
        column = pl.multiple_of(lax.bitwise_xor(d, j) * Q, 128)
        o_copies.append(start(result.at[j], out.at[:, pl.ds(column, Q)], o_sem.at[j]))
    for copy in o_copies:
        copy.wait()


def shards(t, w, acc):
    d, r, col = lax.axis_index("dp"), lax.axis_index("row"), lax.axis_index("col")
    place = jnp.stack([d, r // CORES, r % CORES, col // YH, col % YH]).astype(jnp.int32)

    mine = lax.dynamic_slice(w, (0, d * Q), (KB, Q))
    ys = [send(mine, lambda x, yl, c, z, yh, k=k: (x, yl ^ k, c, z, yh)) for k in (1, 2, 3)]
    t1 = send(t, lambda x, yl, c, z, yh: (x, yl, c, z, 1 - yh))
    t2 = send(t, lambda x, yl, c, z, yh: (x, yl, c, z + 4, yh))
    t3 = send(t, lambda x, yl, c, z, yh: (x, yl, c, z + 4, 1 - yh))
    sw = swap(w)

    g = jnp.concatenate(ys, axis=0)
    xs = [send(g, lambda x, yl, c, z, yh, j=j: (x ^ j, yl, c, z, yh)) for j in (2, 1, 3)]
    xs = [xs[1], xs[0], xs[2]]
    pair = jnp.concatenate([t, t1], axis=1)
    p2 = send(pair, lambda x, yl, c, z, yh: (x, yl, c, z - 2, yh))
    m2 = send(pair, lambda x, yl, c, z, yh: (x, yl, c, z + 2, yh))
    four = jnp.concatenate([t, t1, t2, t3], axis=1)
    vp = send(four, lambda x, yl, c, z, yh: (x, yl, c, z - 1, yh))
    vm = send(four, lambda x, yl, c, z, yh: (x, yl, c, z + 1, yh))
    sg = swap(g)
    ss = [swap(a) for a in xs]

    return pl.pallas_call(
        kernel,
        out_shape=jax.ShapeDtypeStruct((TOK, FF), jnp.bfloat16),
        in_specs=[pl.BlockSpec(memory_space=pltpu.SMEM)] + [pl.BlockSpec(memory_space=pl.ANY)] * 19,
        out_specs=pl.BlockSpec(memory_space=pl.ANY),
        scratch_shapes=[
            pltpu.VMEM((TOK, Z * KB), jnp.bfloat16),
            pltpu.VMEM((X, Z * KB, Q), jnp.bfloat16),
            pltpu.VMEM((X, TOK, Q), jnp.float32),
            pltpu.VMEM((X, TOK, Q), jnp.bfloat16),
            pltpu.SemaphoreType.DMA((16,)),
            pltpu.SemaphoreType.DMA((32,)),
            pltpu.SemaphoreType.DMA((X,)),
            pltpu.SemaphoreType.DMA((X,)),
        ],
        compiler_params=pltpu.CompilerParams(vmem_limit_bytes=32 * 1024 * 1024),
        cost_estimate=pl.CostEstimate(
            flops=2 * TOK * FF * Z * KB, bytes_accessed=13 * 1024 * 1024, transcendentals=TOK * FF
        ),
    )(place, t, t1, t2, t3, vp, vm, p2, m2, w, sw, g, sg, *xs, *ss, acc)


def solution(mesh):
    return jax.shard_map(
        shards,
        mesh=mesh,
        in_specs=(P(("dp", "row"), "col"), P("row", "col"), P(("dp", "row"), "col")),
        out_specs=P(("dp", "row"), "col"),
        check_vma=False,
    )
```

```python
import functools

import jax
import jax.numpy as jnp
from jax import lax
from jax.experimental import pallas as pl
from jax.experimental.pallas import tpu as pltpu
from jax.sharding import PartitionSpec as P

AXES = ("dp", "row", "col")
X, YL, CORES, Z, YH = 4, 4, 2, 8, 2
TOK, KB, FF = 512, 256, 1536
Q = FF // X
HALF = KB // YH


def send(array, to):
    pairs = []
    for x in range(X):
        for yl in range(YL):
            for c in range(CORES):
                for z in range(Z):
                    for yh in range(YH):
                        x2, yl2, c2, z2, yh2 = to(x, yl, c, z, yh)
                        source = (x * YL * CORES + yl * CORES + c) * Z * YH + z * YH + yh
                        target = ((x2 % X) * YL * CORES + yl2 * CORES + c2) * Z * YH + (z2 % Z) * YH + yh2
                        pairs.append((source, target))
    return lax.ppermute(array, AXES, pairs)


def swap(array):
    return send(array, lambda x, yl, c, z, yh: (x, yl, 1 - c, z, yh))


def gelu(v):
    return 0.5 * v * (1.0 + jnp.tanh(0.7978845608028654 * (v + 0.044715 * (v * v * v))))


def kernel(place, tokens, y0, y2, x1, x3, s0, s2, s1, s3, acc, out, t, w, sums, result, t_sem, w_sem, a_sem, o_sem):
    d, c = place[0], place[1]

    def start(source, target, sem):
        copy = pltpu.make_async_copy(source, target, sem)
        copy.start()
        return copy

    t_copies = []
    for z in range(Z):
        side = lax.bitwise_xor(z % CORES, c)
        at = pl.multiple_of(side * (YL * KB) + z // CORES * KB, KB)
        t_copies.append(start(tokens.at[z], t.at[:, pl.ds(at, KB)], t_sem.at[z]))
    pairs = (((y0, s0), (y2, s2)), ((x1, s1), (x3, s3)))
    w_copies, a_copies = [[], []], [[], []]
    for p in range(2):
        for i in range(2):
            j = p + 2 * i
            columns = pl.ds(i * Q, Q)
            for side in range(2):
                w_copies[p].append(start(
                    pairs[p][i][side], w.at[p, pl.ds(side * YL * KB, YL * KB), columns], w_sem.at[j * 2 + side]))
            at = pl.multiple_of(lax.bitwise_xor(d, j) * Q, 128)
            a_copies[p].append(start(acc.at[:, pl.ds(at, Q)], sums.at[p, :, columns], a_sem.at[j]))
    for copy in t_copies:
        copy.wait()
    o_copies = []
    for p in range(2):
        for copy in w_copies[p] + a_copies[p]:
            copy.wait()
        for m in range(0, TOK, 256):
            rows = slice(m, m + 256)
            total = sums[p, rows] + jnp.dot(t[rows], w[p], preferred_element_type=jnp.float32)
            result[p, rows] = gelu(total).astype(jnp.bfloat16)
        for i in range(2):
            at = pl.multiple_of(lax.bitwise_xor(d, p + 2 * i) * Q, 128)
            o_copies.append(start(
                result.at[p, :, pl.ds(i * Q, Q)], out.at[:, pl.ds(at, Q)], o_sem.at[p * 2 + i]))
    for copy in o_copies:
        copy.wait()


def along_y(block, gather):
    groups = [[yl * CORES + c for yl in range(YL)] for c in range(CORES)]
    if gather:
        return lax.all_gather(block, "row", axis=0, tiled=True, axis_index_groups=groups)
    parts = jnp.broadcast_to(block[None], (YL, *block.shape))
    return lax.all_to_all(parts, "row", 0, 0, axis_index_groups=groups).reshape(YL * block.shape[0], block.shape[1])


def along_z(parts):
    groups = [[z * YH + yh for z in range(Z)] for yh in range(YH)]
    return lax.all_to_all(parts, "col", 0, 0, axis_index_groups=groups)


def after(value, *others):
    return lax.optimization_barrier((value, *others))[0]


def shards(t, w, acc):
    d, r, col = lax.axis_index("dp"), lax.axis_index("row"), lax.axis_index("col")
    yh = col % YH
    place = jnp.stack([d, r % CORES]).astype(jnp.int32)

    def quarter(j):
        return lax.dynamic_slice(w, (0, lax.bitwise_xor(d, j) * Q), (KB, Q))

    t1 = send(t, lambda x, yl, c, z, yh: (x, yl, c, z, 1 - yh))
    t0 = jnp.where(yh == 0, jnp.concatenate([t, t1], axis=1), jnp.concatenate([t1, t], axis=1))
    parts = jnp.broadcast_to(t0[None], (Z, *t0.shape))
    tokens = along_z(parts)
    y0 = along_y(quarter(0), True)
    x1 = send(y0, lambda x, yl, c, z, yh: (x ^ 1, yl, c, z, yh))
    x3 = send(y0, lambda x, yl, c, z, yh: (x ^ 3, yl, c, z, yh))
    y2 = along_y(after(quarter(2), y0), True)
    s0, s2, s1, s3 = (swap(a) for a in (y0, y2, x1, x3))

    return pl.pallas_call(
        kernel,
        out_shape=jax.ShapeDtypeStruct((TOK, FF), jnp.bfloat16),
        in_specs=[pl.BlockSpec(memory_space=pltpu.SMEM)] + [pl.BlockSpec(memory_space=pl.ANY)] * 10,
        out_specs=pl.BlockSpec(memory_space=pl.ANY),
        scratch_shapes=[
            pltpu.VMEM((TOK, Z * KB), jnp.bfloat16),
            pltpu.VMEM((2, Z * KB, 2 * Q), jnp.bfloat16),
            pltpu.VMEM((2, TOK, 2 * Q), jnp.float32),
            pltpu.VMEM((2, TOK, 2 * Q), jnp.bfloat16),
            pltpu.SemaphoreType.DMA((Z,)),
            pltpu.SemaphoreType.DMA((8,)),
            pltpu.SemaphoreType.DMA((4,)),
            pltpu.SemaphoreType.DMA((4,)),
        ],
        compiler_params=pltpu.CompilerParams(vmem_limit_bytes=56 * 1024 * 1024),
        cost_estimate=pl.CostEstimate(
            flops=2 * TOK * FF * Z * KB, bytes_accessed=13 * 1024 * 1024, transcendentals=TOK * FF
        ),
    )(place, tokens, y0, y2, x1, x3, s0, s2, s1, s3, acc)


def solution(mesh):
    return jax.shard_map(
        shards,
        mesh=mesh,
        in_specs=(P(("dp", "row"), "col"), P("row", "col"), P(("dp", "row"), "col")),
        out_specs=P(("dp", "row"), "col"),
        check_vma=False,
    )
```

```python
import functools

import jax
import jax.numpy as jnp
from jax import lax
from jax.experimental import pallas as pl
from jax.experimental.pallas import tpu as pltpu
from jax.sharding import PartitionSpec as P

AXES = ("dp", "row", "col")
X, YL, CORES, Z, YH = 4, 4, 2, 8, 2
TOK, KB, FF = 512, 256, 1536
Q = FF // X
HALF = KB // YH


def send(array, to):
    pairs = []
    for x in range(X):
        for yl in range(YL):
            for c in range(CORES):
                for z in range(Z):
                    for yh in range(YH):
                        x2, yl2, c2, z2, yh2 = to(x, yl, c, z, yh)
                        source = (x * YL * CORES + yl * CORES + c) * Z * YH + z * YH + yh
                        target = ((x2 % X) * YL * CORES + yl2 * CORES + c2) * Z * YH + (z2 % Z) * YH + yh2
                        pairs.append((source, target))
    return lax.ppermute(array, AXES, pairs)


def swap(array):
    return send(array, lambda x, yl, c, z, yh: (x, yl, 1 - c, z, yh))


def gelu(v):
    return 0.5 * v * (1.0 + jnp.tanh(0.7978845608028654 * (v + 0.044715 * (v * v * v))))


def kernel(place, tokens, y0, y2, x1, x3, s0, s2, s1, s3, acc, out, w, sums, result, w_sem, a_sem, o_sem):
    d, c = place[0], place[1]
    deep = YL * KB

    def start(source, target, sem):
        copy = pltpu.make_async_copy(source, target, sem)
        copy.start()
        return copy

    def wait(copies):
        for copy in copies:
            copy.wait()

    pairs = (((y0, s0), (y2, s2)), ((x1, s1), (x3, s3)))
    w_copies, a_copies = [], []
    for p in range(2):
        w_copies.append([
            start(pairs[p][i][side], w.at[p, pl.ds(side * deep, deep), pl.ds(i * Q, Q)], w_sem.at[p * 4 + side * 2 + i])
            for side in range(2) for i in range(2)])
        a_copies.append([
            start(acc.at[:, pl.ds(pl.multiple_of(lax.bitwise_xor(d, p + 2 * i) * Q, 128), Q)],
                  sums.at[p, :, pl.ds(i * Q, Q)], a_sem.at[p * 2 + i])
            for i in range(2)])
    o_copies = []
    for p in range(2):
        wait(w_copies[p])
        wait(a_copies[p])
        for m in range(0, TOK, 256):
            rows = slice(m, m + 256)
            total = sums[p, rows]
            for side in range(2):
                for k in range(YL):
                    block = w[p, side * deep + k * KB:side * deep + (k + 1) * KB]
                    total += jnp.dot(
                        tokens[k * CORES + lax.bitwise_xor(side, c), rows], block, preferred_element_type=jnp.float32)
            result[p, rows] = gelu(total).astype(jnp.bfloat16)
        for i in range(2):
            at = pl.multiple_of(lax.bitwise_xor(d, p + 2 * i) * Q, 128)
            o_copies.append(start(
                result.at[p, :, pl.ds(i * Q, Q)], out.at[:, pl.ds(at, Q)], o_sem.at[p * 2 + i]))
    wait(o_copies)


def along_y(block, gather):
    groups = [[yl * CORES + c for yl in range(YL)] for c in range(CORES)]
    if gather:
        return lax.all_gather(block, "row", axis=0, tiled=True, axis_index_groups=groups)
    parts = jnp.broadcast_to(block[None], (YL, *block.shape))
    return lax.all_to_all(parts, "row", 0, 0, axis_index_groups=groups).reshape(YL * block.shape[0], block.shape[1])


def along_z(parts):
    groups = [[z * YH + yh for z in range(Z)] for yh in range(YH)]
    return lax.all_to_all(parts, "col", 0, 0, axis_index_groups=groups)


def after(value, *others):
    return lax.optimization_barrier((value, *others))[0]


def shards(t, w, acc):
    d, r, col = lax.axis_index("dp"), lax.axis_index("row"), lax.axis_index("col")
    yh = col % YH
    place = jnp.stack([d, r % CORES]).astype(jnp.int32)

    def quarter(j):
        return lax.dynamic_slice(w, (0, lax.bitwise_xor(d, j) * Q), (KB, Q))

    t1 = send(t, lambda x, yl, c, z, yh: (x, yl, c, z, 1 - yh))
    t0 = jnp.where(yh == 0, jnp.concatenate([t, t1], axis=1), jnp.concatenate([t1, t], axis=1))
    parts = jnp.broadcast_to(t0[None], (Z, *t0.shape))
    tokens = along_z(parts)
    y0 = along_y(quarter(0), True)
    x1 = send(y0, lambda x, yl, c, z, yh: (x ^ 1, yl, c, z, yh))
    x3 = send(y0, lambda x, yl, c, z, yh: (x ^ 3, yl, c, z, yh))
    y2 = along_y(after(quarter(2), y0), True)
    s0, s2, s1, s3 = (swap(a) for a in (after(y0, y2), y2, x1, x3))

    return pl.pallas_call(
        kernel,
        out_shape=jax.ShapeDtypeStruct((TOK, FF), jnp.bfloat16),
        in_specs=[pl.BlockSpec(memory_space=pltpu.SMEM), pl.BlockSpec(memory_space=pltpu.VMEM)]
        + [pl.BlockSpec(memory_space=pl.ANY)] * 9,
        out_specs=pl.BlockSpec(memory_space=pl.ANY),
        scratch_shapes=[
            pltpu.VMEM((2, Z * KB, 2 * Q), jnp.bfloat16),
            pltpu.VMEM((2, TOK, 2 * Q), jnp.float32),
            pltpu.VMEM((2, TOK, 2 * Q), jnp.bfloat16),
            pltpu.SemaphoreType.DMA((8,)),
            pltpu.SemaphoreType.DMA((4,)),
            pltpu.SemaphoreType.DMA((4,)),
        ],
        compiler_params=pltpu.CompilerParams(vmem_limit_bytes=44 * 1024 * 1024),
        cost_estimate=pl.CostEstimate(
            flops=2 * TOK * FF * Z * KB, bytes_accessed=13 * 1024 * 1024, transcendentals=TOK * FF
        ),
    )(place, tokens, y0, y2, x1, x3, s0, s2, s1, s3, acc)


def solution(mesh):
    return jax.shard_map(
        shards,
        mesh=mesh,
        in_specs=(P(("dp", "row"), "col"), P("row", "col"), P(("dp", "row"), "col")),
        out_specs=P(("dp", "row"), "col"),
        check_vma=False,
    )
```

```python
import functools

import jax
import jax.numpy as jnp
from jax import lax
from jax.experimental import pallas as pl
from jax.experimental.pallas import tpu as pltpu
from jax.sharding import PartitionSpec as P

AXES = ("dp", "row", "col")
X, YL, CORES, Z, YH = 4, 4, 2, 8, 2
TOK, KB, FF = 512, 256, 1536
Q = FF // X
HALF = KB // YH


def send(array, to):
    pairs = []
    for x in range(X):
        for yl in range(YL):
            for c in range(CORES):
                for z in range(Z):
                    for yh in range(YH):
                        x2, yl2, c2, z2, yh2 = to(x, yl, c, z, yh)
                        source = (x * YL * CORES + yl * CORES + c) * Z * YH + z * YH + yh
                        target = ((x2 % X) * YL * CORES + yl2 * CORES + c2) * Z * YH + (z2 % Z) * YH + yh2
                        pairs.append((source, target))
    return lax.ppermute(array, AXES, pairs)


def swap(array):
    return send(array, lambda x, yl, c, z, yh: (x, yl, 1 - c, z, yh))


def gelu(v):
    return 0.5 * v * (1.0 + jnp.tanh(0.7978845608028654 * (v + 0.044715 * (v * v * v))))


def kernel(place, tokens, y0, y2, x1, x3, s0, s2, s1, s3, acc, out, w, sums, result, w_sem, a_sem, o_sem):
    d, c, yh = place[0], place[1], place[2]
    deep = YL * KB

    def start(source, target, sem):
        copy = pltpu.make_async_copy(source, target, sem)
        copy.start()
        return copy

    def wait(copies):
        for copy in copies:
            copy.wait()

    pairs = (((y0, s0), (y2, s2)), ((x1, s1), (x3, s3)))
    w_copies, a_copies = [], []
    for p in range(2):
        w_copies.append([
            start(pairs[p][i][side], w.at[p, pl.ds(side * deep, deep), pl.ds(i * Q, Q)], w_sem.at[p * 4 + side * 2 + i])
            for side in range(2) for i in range(2)])
        a_copies.append([
            start(acc.at[:, pl.ds(pl.multiple_of(lax.bitwise_xor(d, p + 2 * i) * Q, 128), Q)],
                  sums.at[p, :, pl.ds(i * Q, Q)], a_sem.at[p * 2 + i])
            for i in range(2)])
    o_copies = []
    for p in range(2):
        wait(w_copies[p])
        wait(a_copies[p])
        for m in range(0, TOK, 256):
            rows = slice(m, m + 256)
            total = sums[p, rows]
            for side in range(2):
                for k in range(YL):
                    block = w[p, side * deep + k * KB:side * deep + (k + 1) * KB]
                    z = k * CORES + lax.bitwise_xor(side, c)
                    features = jnp.concatenate([tokens[z, yh, rows], tokens[z, 1 - yh, rows]], axis=1)
                    total += jnp.dot(features, block, preferred_element_type=jnp.float32)
            result[p, rows] = gelu(total).astype(jnp.bfloat16)
            for i in range(2):
                at = pl.multiple_of(lax.bitwise_xor(d, p + 2 * i) * Q, 128)
                o_copies.append(start(
                    result.at[p, pl.ds(m, 256), pl.ds(i * Q, Q)], out.at[pl.ds(m, 256), pl.ds(at, Q)],
                    o_sem.at[p * 4 + m // 128 + i]))
    wait(o_copies)


def along_y(block, gather):
    groups = [[yl * CORES + c for yl in range(YL)] for c in range(CORES)]
    if gather:
        return lax.all_gather(block, "row", axis=0, tiled=True, axis_index_groups=groups)
    parts = jnp.broadcast_to(block[None], (YL, *block.shape))
    return lax.all_to_all(parts, "row", 0, 0, axis_index_groups=groups).reshape(YL * block.shape[0], block.shape[1])


def fan(first, second):
    parts = lax.optimization_barrier(jnp.broadcast_to(first[None, None], (Z, 2, *first.shape)))
    block = jnp.broadcast_to(second[None, None], (Z, 1, *second.shape))
    return lax.dynamic_update_slice(parts, block, (0, 1, 0, 0))


def along_z(first, second):
    groups = [[z * YH + yh for z in range(Z)] for yh in range(YH)]
    return lax.all_to_all(fan(first, second), "col", 0, 0, axis_index_groups=groups)


def after(value, *others):
    return lax.optimization_barrier((value, *others))[0]


def shards(t, w, acc):
    d, r, col = lax.axis_index("dp"), lax.axis_index("row"), lax.axis_index("col")
    yh = col % YH
    place = jnp.stack([d, r % CORES, yh]).astype(jnp.int32)

    def quarter(j):
        return lax.dynamic_slice(w, (0, lax.bitwise_xor(d, j) * Q), (KB, Q))

    t1 = send(t, lambda x, yl, c, z, yh: (x, yl, c, z, 1 - yh))
    tokens = along_z(t, t1)
    y0 = along_y(quarter(0), True)
    x1 = send(y0, lambda x, yl, c, z, yh: (x ^ 1, yl, c, z, yh))
    x3 = send(y0, lambda x, yl, c, z, yh: (x ^ 3, yl, c, z, yh))
    y2 = along_y(after(quarter(2), y0), True)
    s0, s2, s1, s3 = (swap(a) for a in (after(y0, y2), y2, x1, x3))

    return pl.pallas_call(
        kernel,
        out_shape=jax.ShapeDtypeStruct((TOK, FF), jnp.bfloat16),
        in_specs=[pl.BlockSpec(memory_space=pltpu.SMEM), pl.BlockSpec(memory_space=pltpu.VMEM)]
        + [pl.BlockSpec(memory_space=pl.ANY)] * 9,
        out_specs=pl.BlockSpec(memory_space=pl.ANY),
        scratch_shapes=[
            pltpu.VMEM((2, Z * KB, 2 * Q), jnp.bfloat16),
            pltpu.VMEM((2, TOK, 2 * Q), jnp.float32),
            pltpu.VMEM((2, TOK, 2 * Q), jnp.bfloat16),
            pltpu.SemaphoreType.DMA((8,)),
            pltpu.SemaphoreType.DMA((4,)),
            pltpu.SemaphoreType.DMA((8,)),
        ],
        compiler_params=pltpu.CompilerParams(vmem_limit_bytes=44 * 1024 * 1024),
        cost_estimate=pl.CostEstimate(
            flops=2 * TOK * FF * Z * KB, bytes_accessed=13 * 1024 * 1024, transcendentals=TOK * FF
        ),
    )(place, tokens, y0, y2, x1, x3, s0, s2, s1, s3, acc)


def solution(mesh):
    return jax.shard_map(
        shards,
        mesh=mesh,
        in_specs=(P(("dp", "row"), "col"), P("row", "col"), P(("dp", "row"), "col")),
        out_specs=P(("dp", "row"), "col"),
        check_vma=False,
    )
```

```python
import functools

import jax
import jax.numpy as jnp
from jax import lax
from jax.experimental import pallas as pl
from jax.experimental.pallas import tpu as pltpu
from jax.sharding import PartitionSpec as P

AXES = ("dp", "row", "col")
X, YL, CORES, Z, YH = 4, 4, 2, 8, 2
TOK, KB, FF = 512, 256, 1536
Q = FF // X
HALF = KB // YH


def send(array, to):
    pairs = []
    for x in range(X):
        for yl in range(YL):
            for c in range(CORES):
                for z in range(Z):
                    for yh in range(YH):
                        x2, yl2, c2, z2, yh2 = to(x, yl, c, z, yh)
                        source = (x * YL * CORES + yl * CORES + c) * Z * YH + z * YH + yh
                        target = ((x2 % X) * YL * CORES + yl2 * CORES + c2) * Z * YH + (z2 % Z) * YH + yh2
                        pairs.append((source, target))
    return lax.ppermute(array, AXES, pairs)


def swap(array):
    return send(array, lambda x, yl, c, z, yh: (x, yl, 1 - c, z, yh))


def gelu(v):
    return 0.5 * v * (1.0 + jnp.tanh(0.7978845608028654 * (v + 0.044715 * (v * v * v))))


def kernel(place, tokens, y0, y2, x1, x3, s0, s2, s1, s3, acc, out, w, sums, result, w_sem, a_sem, o_sem):
    d, c, yh = place[0], place[1], place[2]
    deep = YL * KB

    def start(source, target, sem):
        copy = pltpu.make_async_copy(source, target, sem)
        copy.start()
        return copy

    def wait(copies):
        for copy in copies:
            copy.wait()

    pairs = (((y0, s0), (y2, s2)), ((x1, s1), (x3, s3)))
    w_copies, a_copies = [], []
    for p in range(2):
        for i in range(2):
            w_copies.append([
                start(pairs[p][i][side], w.at[p, pl.ds(side * deep, deep), pl.ds(i * Q, Q)], w_sem.at[p * 4 + side * 2 + i])
                for side in range(2)])
            at = pl.multiple_of(lax.bitwise_xor(d, p + 2 * i) * Q, 128)
            a_copies.append([start(acc.at[:, pl.ds(at, Q)], sums.at[p, :, pl.ds(i * Q, Q)], a_sem.at[p * 2 + i])])
    blocks = [k * CORES + lax.bitwise_xor(side, c) for side in range(2) for k in range(YL)]
    o_copies = []
    for p, first, last, needs in ((0, 0, 256, (0,)), (0, 256, 2 * Q, (1,)), (1, 0, 2 * Q, (2, 3))):
        for q in needs:
            wait(w_copies[q])
            wait(a_copies[q])
        columns = slice(first, last)
        for m in range(0, TOK, 256):
            rows = slice(m, m + 256)
            features = jnp.concatenate([tokens[z, half, rows] for z in blocks for half in (yh, 1 - yh)], axis=1)
            total = sums[p, rows, columns] + jnp.dot(features, w[p, :, columns], preferred_element_type=jnp.float32)
            result[p, rows, columns] = gelu(total).astype(jnp.bfloat16)
            if last == 2 * Q:
                for i in range(2):
                    at = pl.multiple_of(lax.bitwise_xor(d, p + 2 * i) * Q, 128)
                    o_copies.append(start(
                        result.at[p, pl.ds(m, 256), pl.ds(i * Q, Q)], out.at[pl.ds(m, 256), pl.ds(at, Q)],
                        o_sem.at[p * 4 + m // 128 + i]))
    wait(o_copies)


def along_y(block, gather):
    groups = [[yl * CORES + c for yl in range(YL)] for c in range(CORES)]
    if gather:
        return lax.all_gather(block, "row", axis=0, tiled=True, axis_index_groups=groups)
    parts = jnp.broadcast_to(block[None], (YL, *block.shape))
    return lax.all_to_all(parts, "row", 0, 0, axis_index_groups=groups).reshape(YL * block.shape[0], block.shape[1])


def fan(first, second):
    parts = lax.optimization_barrier(jnp.broadcast_to(first[None, None], (Z, 2, *first.shape)))
    block = jnp.broadcast_to(second[None, None], (Z, 1, *second.shape))
    return lax.dynamic_update_slice(parts, block, (0, 1, 0, 0))


def along_z(first, second):
    groups = [[z * YH + yh for z in range(Z)] for yh in range(YH)]
    return lax.all_to_all(fan(first, second), "col", 0, 0, axis_index_groups=groups)


def after(value, *others):
    return lax.optimization_barrier((value, *others))[0]


def shards(t, w, acc):
    d, r, col = lax.axis_index("dp"), lax.axis_index("row"), lax.axis_index("col")
    yh = col % YH
    place = jnp.stack([d, r % CORES, yh]).astype(jnp.int32)

    def quarter(j):
        return lax.dynamic_slice(w, (0, lax.bitwise_xor(d, j) * Q), (KB, Q))

    t1 = send(t, lambda x, yl, c, z, yh: (x, yl, c, z, 1 - yh))
    tokens = along_z(t, t1)
    y0 = along_y(quarter(0), True)
    x1 = send(y0, lambda x, yl, c, z, yh: (x ^ 1, yl, c, z, yh))
    x3 = send(y0, lambda x, yl, c, z, yh: (x ^ 3, yl, c, z, yh))
    y2 = along_y(after(quarter(2), y0), True)
    s0, s2, s1, s3 = (swap(a) for a in (after(y0, y2), y2, x1, x3))

    return pl.pallas_call(
        kernel,
        out_shape=jax.ShapeDtypeStruct((TOK, FF), jnp.bfloat16),
        in_specs=[pl.BlockSpec(memory_space=pltpu.SMEM), pl.BlockSpec(memory_space=pltpu.VMEM)]
        + [pl.BlockSpec(memory_space=pl.ANY)] * 9,
        out_specs=pl.BlockSpec(memory_space=pl.ANY),
        scratch_shapes=[
            pltpu.VMEM((2, Z * KB, 2 * Q), jnp.bfloat16),
            pltpu.VMEM((2, TOK, 2 * Q), jnp.float32),
            pltpu.VMEM((2, TOK, 2 * Q), jnp.bfloat16),
            pltpu.SemaphoreType.DMA((8,)),
            pltpu.SemaphoreType.DMA((4,)),
            pltpu.SemaphoreType.DMA((8,)),
        ],
        compiler_params=pltpu.CompilerParams(vmem_limit_bytes=44 * 1024 * 1024),
        cost_estimate=pl.CostEstimate(
            flops=2 * TOK * FF * Z * KB, bytes_accessed=13 * 1024 * 1024, transcendentals=TOK * FF
        ),
    )(place, tokens, y0, y2, x1, x3, s0, s2, s1, s3, acc)


def solution(mesh):
    return jax.shard_map(
        shards,
        mesh=mesh,
        in_specs=(P(("dp", "row"), "col"), P("row", "col"), P(("dp", "row"), "col")),
        out_specs=P(("dp", "row"), "col"),
        check_vma=False,
    )
```

```python
import functools

import jax
import jax.numpy as jnp
from jax import lax
from jax.experimental import pallas as pl
from jax.experimental.pallas import tpu as pltpu
from jax.sharding import PartitionSpec as P

AXES = ("dp", "row", "col")
X, YL, CORES, Z, YH = 4, 4, 2, 8, 2
TOK, KB, FF = 512, 256, 1536
Q = FF // X
HALF = KB // YH


def send(array, to):
    pairs = []
    for x in range(X):
        for yl in range(YL):
            for c in range(CORES):
                for z in range(Z):
                    for yh in range(YH):
                        x2, yl2, c2, z2, yh2 = to(x, yl, c, z, yh)
                        source = (x * YL * CORES + yl * CORES + c) * Z * YH + z * YH + yh
                        target = ((x2 % X) * YL * CORES + yl2 * CORES + c2) * Z * YH + (z2 % Z) * YH + yh2
                        pairs.append((source, target))
    return lax.ppermute(array, AXES, pairs)


def swap(array):
    return send(array, lambda x, yl, c, z, yh: (x, yl, 1 - c, z, yh))


def gelu(v):
    return 0.5 * v * (1.0 + jnp.tanh(0.7978845608028654 * (v + 0.044715 * (v * v * v))))


def kernel(place, tokens, y0, y2, x1, x3, s0, s2, s1, s3, acc, out, w, sums, result, w_sem, a_sem, o_sem):
    d, c, yh = place[0], place[1], place[2]
    deep = YL * KB

    def start(source, target, sem):
        copy = pltpu.make_async_copy(source, target, sem)
        copy.start()
        return copy

    def wait(copies):
        for copy in copies:
            copy.wait()

    pairs = (((y0, s0), (y2, s2)), ((x1, s1), (x3, s3)))
    w_copies, a_copies = [], []
    for p in range(2):
        for i in range(2):
            w_copies.append([
                start(pairs[p][i][side], w.at[p, pl.ds(side * deep, deep), pl.ds(i * Q, Q)], w_sem.at[p * 4 + side * 2 + i])
                for side in range(2)])
            at = pl.multiple_of(lax.rem(d + p + 2 * i, X) * Q, 128)
            a_copies.append([start(acc.at[:, pl.ds(at, Q)], sums.at[p, :, pl.ds(i * Q, Q)], a_sem.at[p * 2 + i])])
    blocks = [k * CORES + lax.bitwise_xor(side, c) for side in range(2) for k in range(YL)]
    o_copies = []
    for p, first, last, needs in ((0, 0, 256, (0,)), (0, 256, 2 * Q, (1,)), (1, 0, 2 * Q, (2, 3))):
        for q in needs:
            wait(w_copies[q])
            wait(a_copies[q])
        columns = slice(first, last)
        for m in range(0, TOK, 256):
            rows = slice(m, m + 256)
            features = jnp.concatenate([tokens[z, half, rows] for z in blocks for half in (yh, 1 - yh)], axis=1)
            total = sums[p, rows, columns] + jnp.dot(features, w[p, :, columns], preferred_element_type=jnp.float32)
            result[p, rows, columns] = gelu(total).astype(jnp.bfloat16)
            if last == 2 * Q:
                for i in range(2):
                    at = pl.multiple_of(lax.rem(d + p + 2 * i, X) * Q, 128)
                    o_copies.append(start(
                        result.at[p, pl.ds(m, 256), pl.ds(i * Q, Q)], out.at[pl.ds(m, 256), pl.ds(at, Q)],
                        o_sem.at[p * 4 + m // 128 + i]))
    wait(o_copies)


def along_y(block, gather):
    groups = [[yl * CORES + c for yl in range(YL)] for c in range(CORES)]
    if gather:
        return lax.all_gather(block, "row", axis=0, tiled=True, axis_index_groups=groups)
    parts = jnp.broadcast_to(block[None], (YL, *block.shape))
    return lax.all_to_all(parts, "row", 0, 0, axis_index_groups=groups).reshape(YL * block.shape[0], block.shape[1])


def fan(first, second):
    parts = lax.optimization_barrier(jnp.broadcast_to(first[None, None], (Z, 2, *first.shape)))
    block = jnp.broadcast_to(second[None, None], (Z, 1, *second.shape))
    return lax.dynamic_update_slice(parts, block, (0, 1, 0, 0))


def along_z(first, second):
    groups = [[z * YH + yh for z in range(Z)] for yh in range(YH)]
    return lax.all_to_all(fan(first, second), "col", 0, 0, axis_index_groups=groups)


def after(value, *others):
    return lax.optimization_barrier((value, *others))[0]


def shards(t, w, acc):
    d, r, col = lax.axis_index("dp"), lax.axis_index("row"), lax.axis_index("col")
    yh = col % YH
    place = jnp.stack([d, r % CORES, yh]).astype(jnp.int32)

    def quarter(j):
        return lax.dynamic_slice(w, (0, lax.rem(d + j, X) * Q), (KB, Q))

    t1 = send(t, lambda x, yl, c, z, yh: (x, yl, c, z, 1 - yh))
    tokens = along_z(t, t1)
    y0 = along_y(quarter(0), True)
    x1 = send(y0, lambda x, yl, c, z, yh: (x - 1, yl, c, z, yh))
    x3 = send(y0, lambda x, yl, c, z, yh: (x + 1, yl, c, z, yh))
    y2 = along_y(after(quarter(2), y0), True)
    s0, s2, s1, s3 = (swap(a) for a in (after(y0, y2), y2, x1, x3))

    return pl.pallas_call(
        kernel,
        out_shape=jax.ShapeDtypeStruct((TOK, FF), jnp.bfloat16),
        in_specs=[pl.BlockSpec(memory_space=pltpu.SMEM), pl.BlockSpec(memory_space=pltpu.VMEM)]
        + [pl.BlockSpec(memory_space=pl.ANY)] * 9,
        out_specs=pl.BlockSpec(memory_space=pl.ANY),
        scratch_shapes=[
            pltpu.VMEM((2, Z * KB, 2 * Q), jnp.bfloat16),
            pltpu.VMEM((2, TOK, 2 * Q), jnp.float32),
            pltpu.VMEM((2, TOK, 2 * Q), jnp.bfloat16),
            pltpu.SemaphoreType.DMA((8,)),
            pltpu.SemaphoreType.DMA((4,)),
            pltpu.SemaphoreType.DMA((8,)),
        ],
        compiler_params=pltpu.CompilerParams(vmem_limit_bytes=44 * 1024 * 1024),
        cost_estimate=pl.CostEstimate(
            flops=2 * TOK * FF * Z * KB, bytes_accessed=13 * 1024 * 1024, transcendentals=TOK * FF
        ),
    )(place, tokens, y0, y2, x1, x3, s0, s2, s1, s3, acc)


def solution(mesh):
    return jax.shard_map(
        shards,
        mesh=mesh,
        in_specs=(P(("dp", "row"), "col"), P("row", "col"), P(("dp", "row"), "col")),
        out_specs=P(("dp", "row"), "col"),
        check_vma=False,
    )
```
